1024 devices in a mesh: dp: 128 (over z, y_lo, core), fsdp: 8 (over y_hi, x).
Axes of the slice: x: 4, y: 8 (y_hi: 2, y_lo: 4; y = y_hi * 4 + y_lo), z: 16, core: 2. Of those that a mesh axis runs over, the one named last changes fastest.
Arguments:
- acts: bfloat16 [49152, 8192], P('dp', 'fsdp'), may hold values from -6 to 6
- grad_out: bfloat16 [49152, 2048], P('dp'), may hold values from -0.109375 to 0.109375
- basis: bfloat16 [8192, 1024], P('fsdp'), may hold values from -0.0625 to 0.0625
- master: float32 [2048, 8192], P('dp', 'fsdp'), may hold values from -0.12 to 0.12
- exp_avg: float32 [2048, 1024], P('dp', 'fsdp'), may hold values from -1.8 to 1.8
- exp_avg_sq: float32 [2048, 1024], P('dp', 'fsdp'), may hold values from 0.05 to 2
Outputs:
- new_master: float32 [2048, 8192], P('dp', 'fsdp')
- new_weight: bfloat16 [2048, 8192], P(None, 'fsdp')
- new_avg: float32 [2048, 1024], P('dp', 'fsdp')
- new_avg_sq: float32 [2048, 1024], P('dp', 'fsdp')
The draws below stay inside these ranges and needn't reach their ends.
All inputs are finite; a program needn't handle non-finite values.
Results may differ from the reference program's by a relative error of at most 0.0022.
Values may be sent and summed in bfloat16 or wider, within the bound.
A program may use at most 32 MiB of HBM per device.

```python
import math
import jax
import jax.numpy as jnp
from jax import lax

D = 8192
RANK = 1024
TOK_DEV = 384
OUTW = 2048
TOKENS = 49152
N_DP = 128


def spiked(drawn, rng, source, target, parts, factor):
    def block_of(dim):
        return (jnp.arange(drawn.shape[dim]) // (drawn.shape[dim] // parts)).reshape((-1,) + (1,) * (drawn.ndim - 1 - dim))

    first = jax.random.permutation(rng, parts)[block_of(target)]
    second = (block_of(target) + parts // 2) % parts
    return jnp.where((block_of(source) == first) | (block_of(source) == second), factor * drawn, drawn)


def block_scale(key, dims, cuts, least, high):
    def one(axis_at, shards_of):
        draws = jax.random.uniform(jax.random.fold_in(jax.random.fold_in(key, 6), axis_at), (shards_of,), jnp.float32, least / len(cuts), high / len(cuts))
        return jnp.repeat(jnp.exp(draws), dims[axis_at] // shards_of).reshape((-1,) + (1,) * (len(dims) - axis_at - 1))

    loudness = one(*cuts[0])
    for cut in cuts[1:]:
        loudness = loudness * one(*cut)
    return loudness


def bell_draw(stream_key, shape, width, most, shards=(), held_as=jnp.bfloat16):
    result = width * jax.random.normal(stream_key, shape, jnp.float32)
    if shards:
        result = result * block_scale(stream_key, shape, shards, -0.22, 0.18)
    return jnp.clip(result, -most, most).astype(held_as)


def noise_with(own_key, shape, deviation, most, pieces, heavy, kind=jnp.bfloat16):
    drawn = deviation * jax.random.normal(own_key, shape, jnp.float32)
    if pieces:
        drawn = drawn * block_scale(own_key, shape, pieces, -0.22, 0.18)
    return jnp.clip(spiked(drawn, jax.random.fold_in(own_key, 3), *heavy), -most, most).astype(kind)


def setup_inputs(seed: int = 0) -> dict:
    seeds = jax.random.split(jax.random.key(seed), 7)
    return {
        "acts": bell_draw(seeds[0], (TOKENS, D), 1.0, 6.0, ((0, 128), (1, 8))),
        "grad_out": noise_with(seeds[1], (TOKENS, OUTW), (1.0 / (TOK_DEV * N_DP) ** 0.5), 0.109375, ((0, 128),), (0, 1, 128, 5.5)),
        "basis": bell_draw(seeds[2], (D, RANK), D ** -0.5, 0.0625, ((0, 8),)),
        "master": bell_draw(seeds[3], (OUTW, D), 0.02, 0.12, ((0, 128), (1, 8)), jnp.float32),
        "exp_avg": bell_draw(seeds[4], (OUTW, RANK), 0.3, 1.8, ((0, 128), (1, 8)), jnp.float32),
        "exp_avg_sq": jnp.clip(jnp.exp(math.log(2.0) - 3.6888794 * jax.random.uniform(seeds[5], (OUTW, RANK), jnp.float32) ** block_scale(seeds[5], (OUTW, RANK), ((0, 128), (1, 8)), -0.2, 0.2)), 0.05, 2.0),
    }


def reference(acts, grad_out, basis, master, exp_avg, exp_avg_sq):
    proj_acts = jnp.dot(acts, basis, preferred_element_type=jnp.float32).astype(jnp.bfloat16)
    proj_grad = lax.dot_general(grad_out, proj_acts, (((0,), (0,)), ((), ())), preferred_element_type=jnp.float32)
    new_avg = 0.9 * exp_avg + 0.1 * proj_grad
    new_avg_sq = 0.95 * exp_avg_sq + 0.05 * proj_grad * proj_grad
    first_fix = 1.0 - 0.9 ** 20
    second_fix = 1.0 - 0.95 ** 20
    direction = (new_avg / first_fix / (jnp.sqrt(new_avg_sq / second_fix) + 1e-08)).astype(jnp.bfloat16)
    delta = lax.dot_general(direction, basis, (((1,), (1,)), ((), ())), preferred_element_type=jnp.float32)
    new_master = master - 0.0125 * delta
    new_weight = new_master.astype(jnp.bfloat16)
    return (new_master, new_weight, new_avg, new_avg_sq)
```

```python
import functools

import jax
import jax.numpy as jnp
from jax import lax
from jax.experimental import pallas as pl
from jax.experimental.pallas import tpu as pltpu
from jax.sharding import PartitionSpec as P

MESH = pl.DeviceIdType.MESH
LANES = 128
ROWS = 16
F32 = jnp.float32
BF16 = jnp.bfloat16
FAR, NEAR, LAST = 0, 1, 2


def kernel(
    sizes, acts, grad, basis, master, avg, avg_sq,
    new_master, weight, new_avg, new_avg_sq,
    part, rx, cross, ry, grad_v, grad_t, proj, local, from_core, held, ry2, rz2, full_dir,
    g_sem, x_send, x_recv, y_send, y_recv, c_send, c_recv, y2_send, y2_recv,
    z2_send, z2_recv, d_send, d_recv, y4_send, y4_recv, z4_send, z4_recv, s_send, s_recv,
):
    nz, ny, nc, nyh, nx = sizes
    groups = nyh * nx
    half_z = nz // 2
    dp, fs = lax.axis_index("dp"), lax.axis_index("fsdp")
    z, y, c = dp // (ny * nc), (dp // nc) % ny, dp % nc
    yh, x = fs // nx, fs % nx

    def dp_of(z_, y_, c_):
        return (z_ * ny + y_) * nc + c_

    def at_fsdp(f):
        return (dp, f)

    def at_dp(d):
        return (d, fs)

    def remote(src, dst, send, recv, device):
        return pltpu.make_async_remote_copy(
            src_ref=src, dst_ref=dst, send_sem=send, recv_sem=recv,
            device_id=device, device_id_type=MESH,
        )

    def wait_bytes(ref, sem):
        pltpu.make_async_copy(ref, ref, sem).wait()

    sibling = at_dp(dp_of(z, y, nc - 1 - c))

    barrier = pltpu.get_barrier_semaphore()

    def greet(device):
        pl.semaphore_signal(barrier, inc=1, device_id=device, device_id_type=MESH)

    @pl.loop(1, groups)
    def _(k):
        greet(at_fsdp((fs + k) % groups))

    @pl.loop(1, ny)
    def _(k):
        greet(at_dp(dp_of(z, (y + k) % ny, c)))

    @pl.loop(1, nz)
    def _(k):
        greet(at_dp(dp_of((z + k) % nz, y, c)))

    greet(sibling)

    load_grad = pltpu.make_async_copy(grad, grad_v, g_sem)
    load_grad.start()

    half_t = acts.shape[0] // 2

    def project(to_x, to_yh):
        columns = pl.ds(pl.multiple_of((to_yh * nx + to_x) * LANES, LANES), LANES)
        block = jnp.dot(acts[...], basis[:, columns], preferred_element_type=F32)
        part[to_x, to_yh, 0] = block[:half_t]
        part[to_x, to_yh, 1] = block[half_t:]

    def neighbour(way):
        return (x + 1) % nx if way == 0 else (x + nx - 1) % nx

    def x_copy(way, kind, to_yh, src):
        return remote(
            src, rx.at[way, kind, to_yh], x_send.at[way, kind, to_yh],
            x_recv.at[way, kind, to_yh], at_fsdp(yh * nx + neighbour(way)),
        )

    opposite = (x + 2) % nx
    for k in range(nyh):
        to_yh = (yh + 1 + k) % nyh
        project(opposite, to_yh)
        project(neighbour(0), to_yh)
        project(neighbour(1), to_yh)
        if k == 0:
            pl.semaphore_wait(barrier, groups - 1 + ny - 1 + nz - 1 + 1)
        for way in range(2):
            x_copy(way, FAR, to_yh, part.at[opposite, to_yh, way]).start()
        for way in range(2):
            x_copy(way, NEAR, to_yh, part.at[neighbour(way), to_yh, 1 - way]).start()
    for k in range(nyh):
        project(x, (yh + 1 + k) % nyh)

    def relay(to_yh):
        for way in range(2):
            copy = x_copy(way, LAST, to_yh, part.at[neighbour(way), to_yh, way])
            x_copy(way, FAR, to_yh, part.at[opposite, to_yh, way]).wait_recv()
            part[neighbour(way), to_yh, way] += rx[way, FAR, to_yh]
            copy.start()

    def x_total(to_yh, half):
        x_copy(1 - half, NEAR, to_yh, part.at[neighbour(0), to_yh, 0]).wait_recv()
        x_copy(half, LAST, to_yh, part.at[neighbour(0), to_yh, 0]).wait_recv()
        return part[x, to_yh, half] + rx[half, LAST, to_yh] + rx[1 - half, NEAR, to_yh]

    other_yh = (yh + 1) % nyh

    def y_copy(half):
        return remote(
            cross.at[half], ry.at[half], y_send.at[half], y_recv.at[half],
            at_fsdp(other_yh * nx + x),
        )

    relay(other_yh)
    relay(yh)

    load_grad.wait()
    wide = ny * nc * ROWS

    def turn(zz):
        columns = pl.ds(pl.multiple_of(zz * wide, wide), wide)
        turned = grad_v[:, columns].T
        for yy in range(ny):
            for cc in range(nc):
                lo = (yy * nc + cc) * ROWS
                grad_t[cc, yy, zz] = turned[lo : lo + ROWS]

    @pl.loop(0, nz // 2)
    def _(zz):
        turn(zz)

    for half in range(2):
        cross[half] = x_total(other_yh, half)
        y_copy(half).start()

    @pl.loop(nz // 2, nz)
    def _(zz):
        turn(zz)

    for half in range(2):
        total = x_total(yh, half)
        y_copy(half).wait_recv()
        proj[pl.ds(half * half_t, half_t)] = (total + ry[half]).astype(BF16)

    tokens = acts.shape[0]

    def term(cc, yy):
        rows = grad_t[cc, yy].reshape(nz * ROWS, tokens)
        block = jnp.dot(rows, proj[...], preferred_element_type=F32)
        local[cc, yy] = block.reshape(nz, ROWS, LANES)

    def core_copy(yy):
        return remote(
            local.at[nc - 1 - c, yy], from_core.at[yy], c_send.at[yy], c_recv.at[yy], sibling
        )

    @pl.loop(1, ny + 1)
    def _(k):
        yy = (y + k) % ny
        term(nc - 1 - c, yy)
        core_copy(yy).start()

    @pl.loop(1, ny + 1)
    def _(k):
        term(c, (y + k) % ny)

    def y2_copy(k):
        to_y = (y + k) % ny
        return remote(
            held.at[to_y], ry2.at[ny - k], y2_send.at[k], y2_recv.at[ny - k],
            at_dp(dp_of(z, to_y, c)),
        )

    def merge(k):
        yy = (y + k) % ny
        core_copy(yy).wait_recv()
        held[yy] = local[c, yy] + from_core[yy]

    @pl.loop(1, ny)
    def _(k):
        merge(k)
        y2_copy(k).start()

    merge(0)

    @pl.loop(1, ny)
    def _(k):
        y2_copy(ny - k).wait_recv()
        held[y] += ry2[k]

    def z2_copy(k):
        to_z = (z + k) % nz
        return remote(
            held.at[y, to_z], rz2.at[nz - k], z2_send.at[k], z2_recv.at[nz - k],
            at_dp(dp_of(to_z, y, c)),
        )

    @pl.loop(0, nz - 1)
    def _(i):
        z2_copy(half_z + (1 - 2 * (i % 2)) * ((i + 1) // 2)).start()

    proj_grad = held[y, z]
    for k in range(1, nz):
        z2_copy(nz - k).wait_recv()
        proj_grad = proj_grad + rz2[k]

    moment = 0.9 * avg[...] + 0.1 * proj_grad
    moment_sq = 0.95 * avg_sq[...] + 0.05 * proj_grad * proj_grad
    new_avg[...] = moment
    new_avg_sq[...] = moment_sq
    first_fix = 1.0 - 0.9**20
    second_fix = 1.0 - 0.95**20
    direction = moment / first_fix / (jnp.sqrt(moment_sq / second_fix) + 1e-08)

    def rank_block(f):
        return full_dir.at[:, pl.ds(pl.multiple_of(f * LANES, LANES), LANES)]

    rank_block(fs)[...] = direction.astype(BF16)

    def d_copy(k):
        return remote(
            rank_block(fs), rank_block(fs), d_send.at[k], d_recv.at[groups - k],
            at_fsdp((fs + k) % groups),
        )

    @pl.loop(1, groups)
    def _(k):
        d_copy(k).start()

    @pl.loop(1, groups)
    def _(k):
        remote(
            rank_block(fs), rank_block((fs + groups - k) % groups), d_send.at[k],
            d_recv.at[groups - k], at_fsdp((fs + k) % groups),
        ).wait_recv()

    tile = min(256, basis.shape[0])

    @pl.loop(0, basis.shape[0] // tile)
    def _(j):
        features = pl.ds(pl.multiple_of(j * tile, tile), tile)
        delta = lax.dot_general(
            full_dir[...], basis[features, :], (((1,), (1,)), ((), ())),
            preferred_element_type=F32,
        )
        updated = master[:, features] - 0.0125 * delta
        new_master[:, features] = updated
        weight[z, y, c, :, features] = updated.astype(BF16)

    def y4_copy(k):
        return remote(
            weight.at[z, y, c], weight.at[z, y, c], y4_send.at[k], y4_recv.at[ny - k],
            at_dp(dp_of(z, (y + k) % ny, c)),
        )

    def z4_copy(way, step, k):
        back = step - 1
        zz = (z + nz - back) % nz if way == 0 else (z + back) % nz
        to_z = (z + 1) % nz if way == 0 else (z + nz - 1) % nz
        block = weight.at[zz, (y + k) % ny, c]
        return remote(
            block, block, z4_send, z4_recv.at[way, step, k], at_dp(dp_of(to_z, y, c))
        )

    def share(zz, yy):
        block = weight.at[zz, yy, c]
        remote(block, block, s_send, s_recv, sibling).start()

    def last_way(k):
        return 0 if k < ny // 2 else 1

    @pl.loop(1, ny)
    def _(k):
        y4_copy(k).start()

    for k in range(ny):
        if k:
            y4_copy(ny - k).wait_recv()
        for way in range(2):
            if half_z > 1 or last_way(k) == way:
                z4_copy(way, 1, k).start()
        share(z, (y + k) % ny)

    @pl.loop(1, half_z)
    def _(step):
        for k in range(ny):
            for way in range(2):
                z4_copy(way, step, k).wait_recv()
                onward = z4_copy(way, step + 1, k)
                if last_way(k) == way:
                    onward.start()
                else:
                    pl.when(step < half_z - 1)(onward.start)
                share((z + nz - step) % nz if way == 0 else (z + step) % nz, (y + k) % ny)

    for k in range(ny):
        z4_copy(last_way(k), half_z, k).wait_recv()
        share((z + half_z) % nz, (y + k) % ny)

    for way in range(2):
        for kind in range(3):
            for to_yh in range(nyh):
                x_copy(way, kind, to_yh, part.at[0, 0, 0]).wait_send()
    for half in range(2):
        y_copy(half).wait_send()

    @pl.loop(0, ny)
    def _(k):
        core_copy(k).wait_send()

    @pl.loop(1, ny)
    def _(k):
        y2_copy(k).wait_send()
        y4_copy(k).wait_send()

    @pl.loop(1, nz)
    def _(k):
        z2_copy(k).wait_send()

    @pl.loop(1, groups)
    def _(k):
        d_copy(k).wait_send()

    wait_bytes(weight.at[pl.ds(0, nz - 1), :, 0], z4_send)
    wait_bytes(weight.at[:, :, c], s_send)
    wait_bytes(weight.at[:, :, nc - 1 - c], s_recv)


def on_device(sizes, acts, grad_out, basis, master, exp_avg, exp_avg_sq):
    nz, ny, nc, nyh, nx = sizes
    tokens, wide = acts.shape
    groups = nyh * nx
    dma = pltpu.SemaphoreType.DMA
    vmem = pl.BlockSpec(memory_space=pltpu.VMEM)
    shape = jax.ShapeDtypeStruct
    half = tokens // 2
    new_master, weight, new_avg, new_avg_sq = pl.pallas_call(
        functools.partial(kernel, sizes),
        out_shape=(
            shape((ROWS, wide), F32),
            shape((nz, ny, nc, ROWS, wide), BF16),
            shape((ROWS, LANES), F32),
            shape((ROWS, LANES), F32),
        ),
        in_specs=[vmem, pl.BlockSpec(memory_space=pl.ANY), vmem, vmem, vmem, vmem],
        out_specs=[vmem] * 4,
        scratch_shapes=[
            pltpu.VMEM((nx, nyh, 2, half, LANES), F32),
            pltpu.VMEM((2, 3, nyh, half, LANES), F32),
            pltpu.VMEM((2, half, LANES), F32),
            pltpu.VMEM((2, half, LANES), F32),
            pltpu.VMEM(grad_out.shape, BF16),
            pltpu.VMEM((nc, ny, nz, ROWS, tokens), BF16),
            pltpu.VMEM((tokens, LANES), BF16),
            pltpu.VMEM((nc, ny, nz, ROWS, LANES), F32),
            pltpu.VMEM((ny, nz, ROWS, LANES), F32),
            pltpu.VMEM((ny, nz, ROWS, LANES), F32),
            pltpu.VMEM((ny, nz, ROWS, LANES), F32),
            pltpu.VMEM((nz, ROWS, LANES), F32),
            pltpu.VMEM((ROWS, groups * LANES), BF16),
            dma,
            dma((2, 3, nyh)), dma((2, 3, nyh)),
            dma((2,)), dma((2,)),
            dma((ny,)), dma((ny,)),
            dma((ny,)), dma((ny,)),
            dma((nz,)), dma((nz,)),
            dma((groups,)), dma((groups,)),
            dma((ny,)), dma((ny,)),
            dma, dma((2, nz // 2 + 1, ny)),
            dma, dma,
        ],
        compiler_params=pltpu.CompilerParams(
            collective_id=0, has_side_effects=True, vmem_limit_bytes=48 * 1024 * 1024
        ),
        cost_estimate=pl.CostEstimate(
            flops=2 * tokens * LANES * (groups * wide + nz * ny * nc * ROWS),
            bytes_accessed=16 * 1024 * 1024,
            transcendentals=ROWS * LANES,
        ),
        name="galore_step",
    )(acts, grad_out, basis, master, exp_avg, exp_avg_sq)
    return new_master, weight.reshape(nz * ny * nc * ROWS, wide), new_avg, new_avg_sq


def build(mesh, sizes):
    return jax.shard_map(
        functools.partial(on_device, sizes),
        mesh=mesh,
        in_specs=(
            P("dp", "fsdp"),
            P("dp", None),
            P("fsdp", None),
            P("dp", "fsdp"),
            P("dp", "fsdp"),
            P("dp", "fsdp"),
        ),
        out_specs=(P("dp", "fsdp"), P(None, "fsdp"), P("dp", "fsdp"), P("dp", "fsdp")),
        check_vma=False,
    )


def solution(mesh):
    return build(mesh, (16, 4, 2, 2, 4))
```

```python
import functools

import jax
import jax.numpy as jnp
from jax import lax
from jax.experimental import pallas as pl
from jax.experimental.pallas import tpu as pltpu
from jax.sharding import PartitionSpec as P

MESH = pl.DeviceIdType.MESH
LANES = 128
ROWS = 16
F32 = jnp.float32
BF16 = jnp.bfloat16
FAR, NEAR, LAST = 0, 1, 2


def kernel(
    sizes, acts_h, grad, basis_h, master_h, avg_h, avg_sq_h,
    new_master, weight_h, new_avg, new_avg_sq,
    weight, acts, basis, master, avg, avg_sq, part, rx, cross, mid, ry, grad_v, grad_t, proj, local, from_core,
    held_a, held_b, rya, rza, rzb, ryb, basis_t, full_dir,
    in_sems, x_send, x_recv, m_send, m_recv, y_send, y_recv, c_send, c_recv, ya_send, ya_recv,
    za_send, za_recv, zb_send, zb_recv, yb_send, yb_recv, d_send, d_recv, y4_send, y4_recv, z4_send, z4_recv, s_send, s_recv, w_sem,
    b_send, b_recv, by_send, by_recv, t_send, t_recv, v_sem,
):
    nz, ny, nc, nyh, nx = sizes
    groups = nyh * nx
    half_z = nz // 2
    dp, fs = lax.axis_index("dp"), lax.axis_index("fsdp")
    z, y, c = dp // (ny * nc), (dp // nc) % ny, dp % nc
    yh, x = fs // nx, fs % nx

    def dp_of(z_, y_, c_):
        return (z_ * ny + y_) * nc + c_

    def at_fsdp(f):
        return (dp, f)

    def at_dp(d):
        return (d, fs)

    def remote(src, dst, send, recv, device):
        return pltpu.make_async_remote_copy(
            src_ref=src, dst_ref=dst, send_sem=send, recv_sem=recv,
            device_id=device, device_id_type=MESH,
        )

    def wait_bytes(ref, sem):
        pltpu.make_async_copy(ref, ref, sem).wait()

    sibling = at_dp(dp_of(z, y, nc - 1 - c))

    loads = [
        pltpu.make_async_copy(src, dst, in_sems.at[i])
        for i, (src, dst) in enumerate(
            ((acts_h, acts), (basis_h, basis), (grad, grad_v), (master_h, master),
             (avg_h, avg), (avg_sq_h, avg_sq))
        )
    ]
    for load in loads:
        load.start()

    barrier = pltpu.get_barrier_semaphore()

    def greet(device):
        pl.semaphore_signal(barrier, inc=1, device_id=device, device_id_type=MESH)

    @pl.loop(1, groups)
    def _(k):
        greet(at_fsdp((fs + k) % groups))

    @pl.loop(1, ny)
    def _(k):
        greet(at_dp(dp_of(z, (y + k) % ny, c)))

    @pl.loop(1, nz)
    def _(k):
        greet(at_dp(dp_of((z + k) % nz, y, c)))

    line = yh * ny + y
    hop = ny // 2

    def along_y(way):
        there = (line + (hop if way == 0 else nyh * ny - hop)) % (nyh * ny)
        return (dp_of(z, there % ny, c), (there // ny) * nx + x)

    greet(sibling)
    for way in range(2):
        greet(along_y(way))


    quarter = acts.shape[0] // 4
    loads[0].wait()
    loads[1].wait()

    def project(to_x, to_yh):
        columns = pl.ds(pl.multiple_of((to_yh * nx + to_x) * LANES, LANES), LANES)
        block = jnp.dot(acts[...], basis[:, columns], preferred_element_type=F32)
        part[to_x, to_yh] = block.reshape(2, 2, quarter, LANES)

    def neighbour(way):
        return (x + 1) % nx if way == 0 else (x + nx - 1) % nx

    opposite = (x + 2) % nx
    other_yh = (yh + 1) % nyh

    def x_copy(way, kind, to_yh, piece):
        to_x = opposite if kind == FAR else neighbour(way)
        half = 1 - way if kind == NEAR else way
        return remote(
            part.at[to_x, to_yh, half, piece], rx.at[way, kind, to_yh, piece],
            x_send.at[way, kind, to_yh, piece], x_recv.at[way, kind, to_yh, piece],
            at_fsdp(yh * nx + neighbour(way)),
        )

    def send_first(to_yh):
        for kind in (FAR, NEAR):
            for piece in range(2):
                for way in range(2):
                    x_copy(way, kind, to_yh, piece).start()

    def send_last(to_yh):
        for piece in range(2):
            for way in range(2):
                x_copy(way, FAR, to_yh, piece).wait_recv()
                part[neighbour(way), to_yh, way, piece] += rx[way, FAR, to_yh, piece]
                x_copy(way, LAST, to_yh, piece).start()

    def x_total(to_yh, half, piece):
        x_copy(1 - half, NEAR, to_yh, piece).wait_recv()
        x_copy(half, LAST, to_yh, piece).wait_recv()
        return (
            part[x, to_yh, half, piece]
            + rx[half, LAST, to_yh, piece]
            + rx[1 - half, NEAR, to_yh, piece]
        )

    def m_copy(half, piece):
        return remote(
            cross.at[half, piece], mid.at[half, piece], m_send.at[half, piece],
            m_recv.at[half, piece], along_y(half),
        )

    def y_copy(half, piece):
        return remote(
            mid.at[half, piece], ry.at[half, piece], y_send.at[half, piece],
            y_recv.at[half, piece], along_y(half),
        )

    wide = ny * nc * ROWS

    def turn(first, last):
        @pl.loop(first, last)
        def _(zz):
            columns = pl.ds(pl.multiple_of(zz * wide, wide), wide)
            turned = grad_v[:, columns].T
            for yy in range(ny):
                for cc in range(nc):
                    lo = (yy * nc + cc) * ROWS
                    grad_t[cc, yy, zz] = turned[lo : lo + ROWS]

    project(opposite, other_yh)
    project(neighbour(0), other_yh)
    project(neighbour(1), other_yh)
    pl.semaphore_wait(barrier, groups - 1 + ny - 1 + nz - 1 + 1 + 2)
    send_first(other_yh)
    project(x, other_yh)
    send_last(other_yh)
    project(opposite, yh)
    project(neighbour(0), yh)
    project(neighbour(1), yh)
    send_first(yh)
    project(x, yh)
    for piece in range(2):
        for half in range(2):
            cross[half, piece] = x_total(other_yh, half, piece)
            m_copy(half, piece).start()
    send_last(yh)
    loads[2].wait()
    turn(0, nz // 2)
    for piece in range(2):
        for half in range(2):
            m_copy(half, piece).wait_recv()
            y_copy(half, piece).start()
    turn(nz // 2, nz)
    for piece in range(2):
        for half in range(2):
            total = x_total(yh, half, piece)
            y_copy(half, piece).wait_recv()
            rows = pl.ds((2 * half + piece) * quarter, quarter)
            proj[rows] = (total + ry[half, piece]).astype(BF16)
    for load in loads[3:]:
        load.wait()

    tokens = acts.shape[0]

    def term(cc, yy):
        rows = grad_t[cc, yy].reshape(nz * ROWS, tokens)
        block = jnp.dot(rows, proj[...], preferred_element_type=F32)
        local[cc, yy] = block.reshape(nz, ROWS, LANES)

    def core_copy(yy):
        return remote(
            local.at[nc - 1 - c, yy], from_core.at[yy], c_send.at[yy], c_recv.at[yy], sibling
        )

    @pl.loop(1, ny + 1)
    def _(k):
        yy = (y + k) % ny
        term(nc - 1 - c, yy)
        core_copy(yy).start()

    @pl.loop(1, ny + 1)
    def _(k):
        term(c, (y + k) % ny)

    low = ROWS // 2

    def to_y(k):
        return at_dp(dp_of(z, (y + k) % ny, c))

    def to_z(k):
        return at_dp(dp_of((z + k) % nz, y, c))

    def ya_copy(k):
        return remote(
            held_a.at[(y + k) % ny], rya.at[ny - k], ya_send.at[k], ya_recv.at[ny - k], to_y(k)
        )

    def za_copy(k):
        return remote(
            held_a.at[y, (z + k) % nz], rza.at[nz - k], za_send.at[k], za_recv.at[nz - k], to_z(k)
        )

    def zb_copy(k):
        return remote(
            held_b.at[(z + k) % nz], rzb.at[nz - k], zb_send.at[k], zb_recv.at[nz - k], to_z(k)
        )

    def yb_copy(k):
        return remote(
            held_b.at[z, (y + k) % ny], ryb.at[ny - k], yb_send.at[k], yb_recv.at[ny - k], to_y(k)
        )

    def merge(k):
        yy = (y + k) % ny
        core_copy(yy).wait_recv()
        merged = local[c, yy] + from_core[yy]
        held_a[yy] = merged[:, :low]
        held_b[:, yy] = merged[:, low:]

    def far_first(i):
        return half_z + (1 - 2 * (i % 2)) * ((i + 1) // 2)

    @pl.loop(1, ny)
    def _(k):
        merge(k)
        ya_copy(k).start()

    merge(0)

    @pl.loop(0, nz - 1)
    def _(i):
        zb_copy(far_first(i)).start()

    @pl.loop(1, ny)
    def _(k):
        ya_copy(ny - k).wait_recv()
        held_a[y] += rya[k]

    @pl.loop(0, nz - 1)
    def _(i):
        za_copy(far_first(i)).start()

    @pl.loop(0, basis.shape[0] // LANES)
    def _(j):
        features = pl.ds(pl.multiple_of(j * LANES, LANES), LANES)
        basis_t[:, features] = basis[features, :].T

    @pl.loop(1, nz)
    def _(k):
        zb_copy(nz - k).wait_recv()
        held_b[z] += rzb[k]

    @pl.loop(1, ny)
    def _(k):
        yb_copy(k).start()

    grad_a, grad_b = held_a[y, z], held_b[z, y]
    for k in range(1, nz):
        za_copy(nz - k).wait_recv()
        grad_a = grad_a + rza[k]
    for k in range(1, ny):
        yb_copy(ny - k).wait_recv()
        grad_b = grad_b + ryb[k]
    proj_grad = jnp.concatenate([grad_a, grad_b], axis=0)

    moment = 0.9 * avg[...] + 0.1 * proj_grad
    moment_sq = 0.95 * avg_sq[...] + 0.05 * proj_grad * proj_grad
    new_avg[...] = moment
    new_avg_sq[...] = moment_sq
    first_fix = 1.0 - 0.9**20
    second_fix = 1.0 - 0.95**20
    direction = moment / first_fix / (jnp.sqrt(moment_sq / second_fix) + 1e-08)

    def rank_block(f):
        return full_dir.at[:, pl.ds(pl.multiple_of(f * LANES, LANES), LANES)]

    rank_block(fs)[...] = direction.astype(BF16)

    def d_copy(k):
        return remote(
            rank_block(fs), rank_block(fs), d_send.at[k], d_recv.at[groups - k],
            at_fsdp((fs + k) % groups),
        )

    @pl.loop(1, groups)
    def _(k):
        d_copy(k).start()

    @pl.loop(1, groups)
    def _(k):
        remote(
            rank_block(fs), rank_block((fs + groups - k) % groups), d_send.at[k],
            d_recv.at[groups - k], at_fsdp((fs + k) % groups),
        ).wait_recv()

    tile = basis.shape[0] // 4
    first = pl.ds(0, 3 * tile)
    second = pl.ds(3 * tile, tile)

    def update(j):
        features = pl.ds(pl.multiple_of(j * tile, tile), tile)
        delta = jnp.dot(full_dir[...], basis_t[:, features], preferred_element_type=F32)
        updated = master[:, features] - 0.0125 * delta
        new_master[:, features] = updated
        weight[z, y, c, :, features] = updated.astype(BF16)

    def y4_copy(k):
        block = weight.at[z, y, c, :, first]
        return remote(
            block, block, y4_send.at[k], y4_recv.at[ny - k], at_dp(dp_of(z, (y + k) % ny, c))
        )

    def behind(way, step):
        return (z + nz - step) % nz if way == 0 else (z + step) % nz

    def z4_copy(way, stage, ahead, k):
        block = weight.at[behind(way, 2 * (stage - 1)), (y + k) % ny, c, :, first]
        return remote(
            block, block, z4_send, z4_recv.at[way, 2 * (stage - 1) + ahead, k],
            at_dp(dp_of(behind(1 - way, ahead), y, c)),
        )

    def z4_wait(way, step, k):
        wait_bytes(
            weight.at[behind(way, step), (y + k) % ny, c, :, first], z4_recv.at[way, step, k]
        )

    def b_copy(way, stage, ahead):
        block = weight.at[behind(way, 2 * (stage - 1)), y, c, :, second]
        return remote(
            block, block, b_send, b_recv.at[way, 2 * (stage - 1) + ahead],
            at_dp(dp_of(behind(1 - way, ahead), y, c)),
        )

    def b_wait(way, step):
        wait_bytes(weight.at[behind(way, step), y, c, :, second], b_recv.at[way, step])

    def spread(zz):
        block = weight.at[zz, y, c, :, second]

        @pl.loop(1, ny)
        def _(k):
            remote(
                block, block, by_send, by_recv.at[ny - k], at_dp(dp_of(z, (y + k) % ny, c))
            ).start()

    def share(zz):
        block = weight.at[zz, :, c, :, first]
        remote(block, block, s_send, s_recv.at[zz], sibling).start()

    def share_line(yy):
        block = weight.at[:, yy, c, :, second]
        remote(block, block, t_send, t_recv.at[yy], sibling).start()

    def store(zz):
        wait_bytes(weight.at[zz, :, nc - 1 - c, :, first], s_recv.at[zz])
        pltpu.make_async_copy(
            weight.at[zz, :, :, :, first], weight_h.at[zz, :, :, :, first], w_sem
        ).start()

    def store_line(yy):
        wait_bytes(weight.at[:, yy, nc - 1 - c, :, second], t_recv.at[yy])
        pltpu.make_async_copy(
            weight.at[:, yy, :, :, second], weight_h.at[:, yy, :, :, second], v_sem
        ).start()

    def last_way(k):
        return 0 if k < ny // 2 else 1

    stages = half_z // 2

    def onward(way, stage, copy, chosen):
        if chosen:
            copy(way, stage, 2).start()
        else:
            pl.when(stage < stages)(lambda: copy(way, stage, 2).start())
        copy(way, stage, 1).start()

    def z4_onward(way, stage, k):
        onward(way, stage, lambda *args: z4_copy(*args, k), last_way(k) == way)

    update(3)
    for way in range(2):
        onward(way, jnp.int32(1), b_copy, way == 0)
    spread(z)
    pl.loop(0, 3)(update)
    for k in range(ny):
        if k:
            y4_copy(ny - k).wait_recv()
        for way in range(2):
            z4_onward(way, jnp.int32(1), k)
        if not k:
            for j in range(1, ny):
                y4_copy(j).start()
    share(z)

    @pl.loop(1, stages)
    def _(stage):
        for way in range(2):
            b_wait(way, 2 * stage)
            onward(way, stage + 1, b_copy, way == 0)
        for k in range(ny):
            for way in range(2):
                z4_wait(way, 2 * stage, k)
                z4_onward(way, stage + 1, k)
        for way in range(2):
            b_wait(way, 2 * stage - 1)
            for k in range(ny):
                z4_wait(way, 2 * stage - 1, k)
            for back in range(2):
                spread(behind(way, 2 * stage - back))
                share(behind(way, 2 * stage - back))

        @pl.when(stage > 1)
        def _():
            for way in range(2):
                for back in range(2, 4):
                    store(behind(way, 2 * stage - back))

    for way in range(2):
        b_wait(way, half_z - 1)
        spread(behind(way, half_z - 1))
    b_wait(0, half_z)
    spread(behind(0, half_z))
    share_line(y)
    for way in range(2):
        for k in range(ny):
            z4_wait(way, half_z - 1, k)
        share(behind(way, half_z - 1))
    for k in range(ny):
        z4_wait(last_way(k), half_z, k)
    share(behind(0, half_z))
    store(z)
    for way in range(2):
        for step in range(max(half_z - 3, 1), half_z):
            store(behind(way, step))
    for k in range(1, ny):
        yy = (y + k) % ny
        wait_bytes(weight.at[:, yy, c, :, second], by_recv.at[k])
        share_line(yy)
    store(behind(0, half_z))
    for k in range(ny):
        store_line((y + k) % ny)

    for way in range(2):
        for kind in range(3):
            for to_yh in range(nyh):
                for piece in range(2):
                    x_copy(way, kind, to_yh, piece).wait_send()
    for half in range(2):
        for piece in range(2):
            m_copy(half, piece).wait_send()
            y_copy(half, piece).wait_send()

    @pl.loop(0, ny)
    def _(k):
        core_copy(k).wait_send()

    @pl.loop(1, ny)
    def _(k):
        ya_copy(k).wait_send()
        yb_copy(k).wait_send()
        y4_copy(k).wait_send()

    @pl.loop(1, nz)
    def _(k):
        za_copy(k).wait_send()
        zb_copy(k).wait_send()

    @pl.loop(1, groups)
    def _(k):
        d_copy(k).wait_send()

    wait_bytes(weight.at[pl.ds(0, nz - 1), :, 0, :, first], z4_send)
    wait_bytes(weight.at[pl.ds(0, nz - 1), 0, 0, :, second], b_send)
    wait_bytes(weight.at[:, pl.ds(0, ny - 1), 0, :, second], by_send)
    wait_bytes(weight.at[:, :, 0, :, first], s_send)
    wait_bytes(weight.at[:, :, 0, :, second], t_send)
    wait_bytes(weight.at[:, :, :, :, first], w_sem)
    wait_bytes(weight.at[:, :, :, :, second], v_sem)


def deliver(master, weight, avg, avg_sq, *refs):
    outs, (staged, *small, sems) = refs[:4], refs[4:]
    moves = [(master, small[0], outs[0]), (avg, small[1], outs[2]), (avg_sq, small[2], outs[3])]
    moves += [(weight.at[i], staged.at[i], outs[1].at[i]) for i in range(weight.shape[0])]
    reads = [pltpu.make_async_copy(m[0], m[1], sems.at[0, i]) for i, m in enumerate(moves)]
    writes = [pltpu.make_async_copy(m[1], m[2], sems.at[1, i]) for i, m in enumerate(moves)]
    for read in reads:
        read.start()
    for read, write in zip(reads, writes):
        read.wait()
        write.start()
    for write in writes:
        write.wait()


def on_device(sizes, acts, grad_out, basis, master, exp_avg, exp_avg_sq):
    nz, ny, nc, nyh, nx = sizes
    tokens, wide = acts.shape
    groups = nyh * nx
    dma = pltpu.SemaphoreType.DMA
    vmem = pl.BlockSpec(memory_space=pltpu.VMEM)
    hbm = pl.BlockSpec(memory_space=pltpu.HBM)
    shape = jax.ShapeDtypeStruct
    quarter = tokens // 4
    results = pl.pallas_call(
        functools.partial(kernel, sizes),
        out_shape=(
            shape((ROWS, wide), F32),
            shape((nz, ny, nc, ROWS, wide), BF16),
            shape((ROWS, LANES), F32),
            shape((ROWS, LANES), F32),
        ),
        in_specs=[hbm] * 6,
        out_specs=[vmem, hbm, vmem, vmem],
        scratch_shapes=[
            pltpu.VMEM((nz, ny, nc, ROWS, wide), BF16),
            pltpu.VMEM(acts.shape, BF16),
            pltpu.VMEM(basis.shape, BF16),
            pltpu.VMEM(master.shape, F32),
            pltpu.VMEM(exp_avg.shape, F32),
            pltpu.VMEM(exp_avg_sq.shape, F32),
            pltpu.VMEM((nx, nyh, 2, 2, quarter, LANES), F32),
            pltpu.VMEM((2, 3, nyh, 2, quarter, LANES), F32),
            pltpu.VMEM((2, 2, quarter, LANES), F32),
            pltpu.VMEM((2, 2, quarter, LANES), F32),
            pltpu.VMEM((2, 2, quarter, LANES), F32),
            pltpu.VMEM(grad_out.shape, BF16),
            pltpu.VMEM((nc, ny, nz, ROWS, tokens), BF16),
            pltpu.VMEM((tokens, LANES), BF16),
            pltpu.VMEM((nc, ny, nz, ROWS, LANES), F32),
            pltpu.VMEM((ny, nz, ROWS, LANES), F32),
            pltpu.VMEM((ny, nz, ROWS // 2, LANES), F32),
            pltpu.VMEM((nz, ny, ROWS // 2, LANES), F32),
            pltpu.VMEM((ny, nz, ROWS // 2, LANES), F32),
            pltpu.VMEM((nz, ROWS // 2, LANES), F32),
            pltpu.VMEM((nz, ny, ROWS // 2, LANES), F32),
            pltpu.VMEM((ny, ROWS // 2, LANES), F32),
            pltpu.VMEM((groups * LANES, wide), BF16),
            pltpu.VMEM((ROWS, groups * LANES), BF16),
            dma((6,)),
            dma((2, 3, nyh, 2)), dma((2, 3, nyh, 2)),
            dma((2, 2)), dma((2, 2)),
            dma((2, 2)), dma((2, 2)),
            dma((ny,)), dma((ny,)),
            dma((ny,)), dma((ny,)),
            dma((nz,)), dma((nz,)),
            dma((nz,)), dma((nz,)),
            dma((ny,)), dma((ny,)),
            dma((groups,)), dma((groups,)),
            dma((ny,)), dma((ny,)),
            dma, dma((2, nz // 2 + 1, ny)),
            dma, dma((nz,)), dma,
            dma, dma((2, nz // 2 + 1)), dma, dma((ny,)), dma, dma((ny,)), dma,
        ],
        compiler_params=pltpu.CompilerParams(
            collective_id=0, has_side_effects=True, vmem_limit_bytes=58 * 1024 * 1024
        ),
        cost_estimate=pl.CostEstimate(
            flops=2 * tokens * LANES * (groups * wide + nz * ny * nc * ROWS),
            bytes_accessed=16 * 1024 * 1024,
            transcendentals=ROWS * LANES,
        ),
        name="galore_step",
    )(acts, grad_out, basis, master, exp_avg, exp_avg_sq)
    new_master, weight, new_avg, new_avg_sq = pl.pallas_call(
        deliver,
        out_shape=[shape(r.shape, r.dtype) for r in results],
        in_specs=[hbm] * 4,
        out_specs=[hbm] * 4,
        scratch_shapes=[pltpu.VMEM(results[i].shape, results[i].dtype) for i in (1, 0, 2, 3)]
        + [dma((2, 3 + nz))],
        compiler_params=pltpu.CompilerParams(vmem_limit_bytes=58 * 1024 * 1024),
        name="deliver",
    )(*results)
    return new_master, weight.reshape(nz * ny * nc * ROWS, wide), new_avg, new_avg_sq


def build(mesh, sizes):
    return jax.shard_map(
        functools.partial(on_device, sizes),
        mesh=mesh,
        in_specs=(
            P("dp", "fsdp"),
            P("dp", None),
            P("fsdp", None),
            P("dp", "fsdp"),
            P("dp", "fsdp"),
            P("dp", "fsdp"),
        ),
        out_specs=(P("dp", "fsdp"), P(None, "fsdp"), P("dp", "fsdp"), P("dp", "fsdp")),
        check_vma=False,
    )


def solution(mesh):
    return build(mesh, (16, 4, 2, 2, 4))
```

```python
import functools

import jax
import jax.numpy as jnp
from jax import lax
from jax.experimental import pallas as pl
from jax.experimental.pallas import tpu as pltpu
from jax.sharding import PartitionSpec as P

MESH = pl.DeviceIdType.MESH
LANES = 128
ROWS = 16
F32 = jnp.float32
BF16 = jnp.bfloat16
FAR, NEAR, LAST = 0, 1, 2
FIRST_HOPS = (2, 1, 2, 1, 2)


def kernel(
    sizes, acts_h, grad, basis_h, master_h, avg_h, avg_sq_h,
    new_master, weight_h, new_avg, new_avg_sq,
    weight, acts, basis, master, avg, avg_sq, part, rx, cross, ry, grad_v, grad_t, proj, local, from_core,
    held_a, held_b, rya, rza, rzb, ryb, basis_t, full_dir,
    in_sems, x_send, x_recv, y_send, y_recv, c_send, c_recv, ya_send, ya_recv,
    za_send, za_recv, zb_send, zb_recv, yb_send, yb_recv, d_send, d_recv, y4_send, y4_recv, z4_send, z4_recv, s_send, s_recv, w_sem,
    b_send, b_recv, by_send, by_recv, t_send, t_recv, v_sem,
):
    nz, ny, nc, nyh, nx = sizes
    groups = nyh * nx
    half_z = nz // 2
    dp, fs = lax.axis_index("dp"), lax.axis_index("fsdp")
    z, y, c = dp // (ny * nc), (dp // nc) % ny, dp % nc
    yh, x = fs // nx, fs % nx

    def dp_of(z_, y_, c_):
        return (z_ * ny + y_) * nc + c_

    def at_fsdp(f):
        return (dp, f)

    def at_dp(d):
        return (d, fs)

    def remote(src, dst, send, recv, device):
        return pltpu.make_async_remote_copy(
            src_ref=src, dst_ref=dst, send_sem=send, recv_sem=recv,
            device_id=device, device_id_type=MESH,
        )

    def wait_bytes(ref, sem):
        pltpu.make_async_copy(ref, ref, sem).wait()

    sibling = at_dp(dp_of(z, y, nc - 1 - c))

    loads = [
        pltpu.make_async_copy(src, dst, in_sems.at[i])
        for i, (src, dst) in enumerate(
            ((acts_h, acts), (basis_h, basis), (grad, grad_v), (master_h, master),
             (avg_h, avg), (avg_sq_h, avg_sq))
        )
    ]
    for load in loads:
        load.start()

    barrier = pltpu.get_barrier_semaphore()

    def greet(device):
        pl.semaphore_signal(barrier, inc=1, device_id=device, device_id_type=MESH)

    @pl.loop(1, groups)
    def _(k):
        greet(at_fsdp((fs + k) % groups))

    @pl.loop(1, ny)
    def _(k):
        greet(at_dp(dp_of(z, (y + k) % ny, c)))

    @pl.loop(1, nz)
    def _(k):
        greet(at_dp(dp_of((z + k) % nz, y, c)))

    greet(sibling)


    quarter = acts.shape[0] // 4
    loads[0].wait()
    loads[1].wait()

    def project(to_x, to_yh):
        columns = pl.ds(pl.multiple_of((to_yh * nx + to_x) * LANES, LANES), LANES)
        block = jnp.dot(acts[...], basis[:, columns], preferred_element_type=F32)
        part[to_x, to_yh] = block.reshape(2, 2, quarter, LANES)

    def neighbour(way):
        return (x + 1) % nx if way == 0 else (x + nx - 1) % nx

    opposite = (x + 2) % nx
    other_yh = (yh + 1) % nyh

    def x_copy(way, kind, to_yh, piece):
        to_x = opposite if kind == FAR else neighbour(way)
        half = 1 - way if kind == NEAR else way
        return remote(
            part.at[to_x, to_yh, half, piece], rx.at[way, kind, to_yh, piece],
            x_send.at[way, kind, to_yh, piece], x_recv.at[way, kind, to_yh, piece],
            at_fsdp(yh * nx + neighbour(way)),
        )

    def send_first(to_yh):
        for kind in (FAR, NEAR):
            for piece in range(2):
                for way in range(2):
                    x_copy(way, kind, to_yh, piece).start()

    def send_last(to_yh):
        for piece in range(2):
            for way in range(2):
                x_copy(way, FAR, to_yh, piece).wait_recv()
                part[neighbour(way), to_yh, way, piece] += rx[way, FAR, to_yh, piece]
                x_copy(way, LAST, to_yh, piece).start()

    def x_total(to_yh, half, piece):
        x_copy(1 - half, NEAR, to_yh, piece).wait_recv()
        x_copy(half, LAST, to_yh, piece).wait_recv()
        return (
            part[x, to_yh, half, piece]
            + rx[half, LAST, to_yh, piece]
            + rx[1 - half, NEAR, to_yh, piece]
        )

    def y_copy(half, piece):
        return remote(
            cross.at[half, piece], ry.at[half, piece], y_send.at[half, piece],
            y_recv.at[half, piece], at_fsdp(other_yh * nx + x),
        )

    wide = ny * nc * ROWS

    def turn(first, last):
        @pl.loop(first, last)
        def _(zz):
            columns = pl.ds(pl.multiple_of(zz * wide, wide), wide)
            turned = grad_v[:, columns].T
            for yy in range(ny):
                for cc in range(nc):
                    lo = (yy * nc + cc) * ROWS
                    grad_t[cc, yy, zz] = turned[lo : lo + ROWS]

    project(opposite, other_yh)
    project(neighbour(0), other_yh)
    project(neighbour(1), other_yh)
    pl.semaphore_wait(barrier, groups - 1 + ny - 1 + nz - 1 + 1)
    send_first(other_yh)
    project(x, other_yh)
    send_last(other_yh)
    project(opposite, yh)
    project(neighbour(0), yh)
    project(neighbour(1), yh)
    send_first(yh)
    project(x, yh)
    for piece in range(2):
        for half in range(2):
            cross[half, piece] = x_total(other_yh, half, piece)
            y_copy(half, piece).start()
    send_last(yh)
    loads[2].wait()
    turn(0, nz // 2)
    turn(nz // 2, nz)
    for piece in range(2):
        for half in range(2):
            total = x_total(yh, half, piece)
            y_copy(half, piece).wait_recv()
            rows = pl.ds((2 * half + piece) * quarter, quarter)
            proj[rows] = (total + ry[half, piece]).astype(BF16)
    for load in loads[3:]:
        load.wait()

    tokens = acts.shape[0]

    def term(cc, yy):
        rows = grad_t[cc, yy].reshape(nz * ROWS, tokens)
        block = jnp.dot(rows, proj[...], preferred_element_type=F32)
        local[cc, yy] = block.reshape(nz, ROWS, LANES)

    def core_copy(yy):
        return remote(
            local.at[nc - 1 - c, yy], from_core.at[yy], c_send.at[yy], c_recv.at[yy], sibling
        )

    @pl.loop(1, ny + 1)
    def _(k):
        yy = (y + k) % ny
        term(nc - 1 - c, yy)
        core_copy(yy).start()

    @pl.loop(1, ny + 1)
    def _(k):
        term(c, (y + k) % ny)

    low = ROWS // 2

    def to_y(k):
        return at_dp(dp_of(z, (y + k) % ny, c))

    def to_z(k):
        return at_dp(dp_of((z + k) % nz, y, c))

    def ya_copy(k):
        return remote(
            held_a.at[(y + k) % ny], rya.at[ny - k], ya_send.at[k], ya_recv.at[ny - k], to_y(k)
        )

    def za_copy(k):
        return remote(
            held_a.at[y, (z + k) % nz], rza.at[nz - k], za_send.at[k], za_recv.at[nz - k], to_z(k)
        )

    def zb_copy(k):
        return remote(
            held_b.at[(z + k) % nz], rzb.at[nz - k], zb_send.at[k], zb_recv.at[nz - k], to_z(k)
        )

    def yb_copy(k):
        return remote(
            held_b.at[z, (y + k) % ny], ryb.at[ny - k], yb_send.at[k], yb_recv.at[ny - k], to_y(k)
        )

    def merge(k):
        yy = (y + k) % ny
        core_copy(yy).wait_recv()
        merged = local[c, yy] + from_core[yy]
        held_a[yy] = merged[:, :low]
        held_b[:, yy] = merged[:, low:]

    def far_first(i):
        return half_z + (1 - 2 * (i % 2)) * ((i + 1) // 2)

    @pl.loop(1, ny)
    def _(k):
        merge(k)
        ya_copy(k).start()

    merge(0)

    @pl.loop(0, nz - 1)
    def _(i):
        zb_copy(far_first(i)).start()

    @pl.loop(1, ny)
    def _(k):
        ya_copy(ny - k).wait_recv()
        held_a[y] += rya[k]

    @pl.loop(0, nz - 1)
    def _(i):
        za_copy(far_first(i)).start()

    @pl.loop(0, basis.shape[0] // LANES)
    def _(j):
        features = pl.ds(pl.multiple_of(j * LANES, LANES), LANES)
        basis_t[:, features] = basis[features, :].T

    @pl.loop(1, nz)
    def _(k):
        zb_copy(nz - k).wait_recv()
        held_b[z] += rzb[k]

    @pl.loop(1, ny)
    def _(k):
        yb_copy(k).start()

    grad_a, grad_b = held_a[y, z], held_b[z, y]
    for k in range(1, nz):
        za_copy(nz - k).wait_recv()
        grad_a = grad_a + rza[k]
    for k in range(1, ny):
        yb_copy(ny - k).wait_recv()
        grad_b = grad_b + ryb[k]
    proj_grad = jnp.concatenate([grad_a, grad_b], axis=0)

    moment = 0.9 * avg[...] + 0.1 * proj_grad
    moment_sq = 0.95 * avg_sq[...] + 0.05 * proj_grad * proj_grad
    new_avg[...] = moment
    new_avg_sq[...] = moment_sq
    first_fix = 1.0 - 0.9**20
    second_fix = 1.0 - 0.95**20
    direction = moment / first_fix / (jnp.sqrt(moment_sq / second_fix) + 1e-08)

    def rank_block(f):
        return full_dir.at[:, pl.ds(pl.multiple_of(f * LANES, LANES), LANES)]

    rank_block(fs)[...] = direction.astype(BF16)

    def d_copy(k):
        return remote(
            rank_block(fs), rank_block(fs), d_send.at[k], d_recv.at[groups - k],
            at_fsdp((fs + k) % groups),
        )

    @pl.loop(1, groups)
    def _(k):
        d_copy(k).start()

    @pl.loop(1, groups)
    def _(k):
        remote(
            rank_block(fs), rank_block((fs + groups - k) % groups), d_send.at[k],
            d_recv.at[groups - k], at_fsdp((fs + k) % groups),
        ).wait_recv()

    tiles = basis.shape[0] // LANES
    cut = tiles * 5 // 8
    first = pl.ds(0, cut * LANES)
    second = pl.ds(cut * LANES, (tiles - cut) * LANES)

    def update(j):
        features = pl.ds(pl.multiple_of(j * LANES, LANES), LANES)
        delta = jnp.dot(full_dir[...], basis_t[:, features], preferred_element_type=F32)
        updated = master[:, features] - 0.0125 * delta
        new_master[:, features] = updated
        weight[z, y, c, :, features] = updated.astype(BF16)

    def y4_copy(k):
        block = weight.at[z, y, c, :, first]
        return remote(
            block, block, y4_send.at[k], y4_recv.at[ny - k], at_dp(dp_of(z, (y + k) % ny, c))
        )

    def behind(way, step):
        return (z + nz - step) % nz if way == 0 else (z + step) % nz

    def ring(hops):
        starts = [sum(hops[:i]) for i in range(len(hops))]
        return [(at, [at + ahead for ahead in range(hop, 0, -1)]) for at, hop in zip(starts, hops)]

    ring_a = ring(FIRST_HOPS if half_z == 8 else (2,) * (half_z // 2))
    ring_b = ring((2,) * (half_z // 2))

    def z4_send_on(way, at, steps, k):
        block = weight.at[behind(way, at), (y + k) % ny, c, :, first]
        for step in steps:
            if step < half_z or way == last_way(k):
                remote(
                    block, block, z4_send, z4_recv.at[way, step, k],
                    at_dp(dp_of(behind(1 - way, step - at), y, c)),
                ).start()

    def z4_wait(way, step, k):
        wait_bytes(
            weight.at[behind(way, step), (y + k) % ny, c, :, first], z4_recv.at[way, step, k]
        )

    def b_send_on(way, at, steps):
        block = weight.at[behind(way, at), y, c, :, second]
        for step in steps:
            if step < half_z or way == 0:
                remote(
                    block, block, b_send, b_recv.at[way, step],
                    at_dp(dp_of(behind(1 - way, step - at), y, c)),
                ).start()

    def b_wait(way, step):
        wait_bytes(weight.at[behind(way, step), y, c, :, second], b_recv.at[way, step])

    def spread(zz):
        block = weight.at[zz, y, c, :, second]

        @pl.loop(1, ny)
        def _(k):
            remote(
                block, block, by_send, by_recv.at[ny - k], at_dp(dp_of(z, (y + k) % ny, c))
            ).start()

    def share(zz):
        block = weight.at[zz, :, c, :, first]
        remote(block, block, s_send, s_recv.at[zz], sibling).start()

    def share_line(yy):
        block = weight.at[:, yy, c, :, second]
        remote(block, block, t_send, t_recv.at[yy], sibling).start()

    def store(zz):
        wait_bytes(weight.at[zz, :, nc - 1 - c, :, first], s_recv.at[zz])
        pltpu.make_async_copy(
            weight.at[zz, :, :, :, first], weight_h.at[zz, :, :, :, first], w_sem
        ).start()

    def store_line(yy):
        wait_bytes(weight.at[:, yy, nc - 1 - c, :, second], t_recv.at[yy])
        pltpu.make_async_copy(
            weight.at[:, yy, :, :, second], weight_h.at[:, yy, :, :, second], v_sem
        ).start()

    def last_way(k):
        return 0 if k < ny // 2 else 1

    def each_way(step):
        return range(2) if step < half_z else range(1)

    pl.loop(cut, tiles)(update)
    for way in range(2):
        b_send_on(way, *ring_b[0])
    spread(z)
    pl.loop(0, cut)(update)
    for k in range(ny):
        if k:
            y4_copy(ny - k).wait_recv()
        for way in range(2):
            z4_send_on(way, *ring_a[0], k)
        if not k:
            for j in range(1, ny):
                y4_copy(j).start()
    share(z)

    queue_b = list(zip(ring_b, ring_b[1:] + [None]))
    stored = []
    for (_, steps), onward in zip(ring_a, ring_a[1:] + [None]):
        while queue_b and queue_b[0][0][1][0] <= max(steps[0], 2):
            (_, b_steps), b_onward = queue_b.pop(0)
            for step in b_steps:
                for way in each_way(step):
                    b_wait(way, step)
                    if b_onward and step == b_onward[0]:
                        b_send_on(way, *b_onward)
            for step in b_steps:
                for way in each_way(step):
                    spread(behind(way, step))
        for step in steps:
            for k in range(ny):
                for way in range(2):
                    if step < half_z or way == last_way(k):
                        z4_wait(way, step, k)
                        if onward and step == onward[0]:
                            z4_send_on(way, *onward, k)
        for step in steps:
            for way in each_way(step):
                share(behind(way, step))
        if not onward:
            share_line(y)
        while len(stored) > 4:
            store(stored.pop(0))
        stored += [behind(way, step) for step in reversed(steps) for way in each_way(step)]

    store(z)
    for zz in stored:
        store(zz)
    for k in range(1, ny):
        yy = (y + k) % ny
        wait_bytes(weight.at[:, yy, c, :, second], by_recv.at[k])
        share_line(yy)
    for k in range(ny):
        store_line((y + k) % ny)

    for way in range(2):
        for kind in range(3):
            for to_yh in range(nyh):
                for piece in range(2):
                    x_copy(way, kind, to_yh, piece).wait_send()
    for half in range(2):
        for piece in range(2):
            y_copy(half, piece).wait_send()

    @pl.loop(0, ny)
    def _(k):
        core_copy(k).wait_send()

    @pl.loop(1, ny)
    def _(k):
        ya_copy(k).wait_send()
        yb_copy(k).wait_send()
        y4_copy(k).wait_send()

    @pl.loop(1, nz)
    def _(k):
        za_copy(k).wait_send()
        zb_copy(k).wait_send()

    @pl.loop(1, groups)
    def _(k):
        d_copy(k).wait_send()

    wait_bytes(weight.at[pl.ds(0, nz - 1), :, 0, :, first], z4_send)
    wait_bytes(weight.at[pl.ds(0, nz - 1), 0, 0, :, second], b_send)
    wait_bytes(weight.at[:, pl.ds(0, ny - 1), 0, :, second], by_send)
    wait_bytes(weight.at[:, :, 0, :, first], s_send)
    wait_bytes(weight.at[:, :, 0, :, second], t_send)
    wait_bytes(weight.at[:, :, :, :, first], w_sem)
    wait_bytes(weight.at[:, :, :, :, second], v_sem)


def deliver(master, weight, avg, avg_sq, *refs):
    outs, (staged, *small, sems) = refs[:4], refs[4:]
    moves = [(master, small[0], outs[0]), (avg, small[1], outs[2]), (avg_sq, small[2], outs[3])]
    moves += [(weight.at[i], staged.at[i], outs[1].at[i]) for i in range(weight.shape[0])]
    reads = [pltpu.make_async_copy(m[0], m[1], sems.at[0, i]) for i, m in enumerate(moves)]
    writes = [pltpu.make_async_copy(m[1], m[2], sems.at[1, i]) for i, m in enumerate(moves)]
    for read in reads:
        read.start()
    for read, write in zip(reads, writes):
        read.wait()
        write.start()
    for write in writes:
        write.wait()


def on_device(sizes, acts, grad_out, basis, master, exp_avg, exp_avg_sq):
    nz, ny, nc, nyh, nx = sizes
    tokens, wide = acts.shape
    groups = nyh * nx
    dma = pltpu.SemaphoreType.DMA
    vmem = pl.BlockSpec(memory_space=pltpu.VMEM)
    hbm = pl.BlockSpec(memory_space=pltpu.HBM)
    shape = jax.ShapeDtypeStruct
    quarter = tokens // 4
    results = pl.pallas_call(
        functools.partial(kernel, sizes),
        out_shape=(
            shape((ROWS, wide), F32),
            shape((nz, ny, nc, ROWS, wide), BF16),
            shape((ROWS, LANES), F32),
            shape((ROWS, LANES), F32),
        ),
        in_specs=[hbm] * 6,
        out_specs=[vmem, hbm, vmem, vmem],
        scratch_shapes=[
            pltpu.VMEM((nz, ny, nc, ROWS, wide), BF16),
            pltpu.VMEM(acts.shape, BF16),
            pltpu.VMEM(basis.shape, BF16),
            pltpu.VMEM(master.shape, F32),
            pltpu.VMEM(exp_avg.shape, F32),
            pltpu.VMEM(exp_avg_sq.shape, F32),
            pltpu.VMEM((nx, nyh, 2, 2, quarter, LANES), F32),
            pltpu.VMEM((2, 3, nyh, 2, quarter, LANES), F32),
            pltpu.VMEM((2, 2, quarter, LANES), F32),
            pltpu.VMEM((2, 2, quarter, LANES), F32),
            pltpu.VMEM(grad_out.shape, BF16),
            pltpu.VMEM((nc, ny, nz, ROWS, tokens), BF16),
            pltpu.VMEM((tokens, LANES), BF16),
            pltpu.VMEM((nc, ny, nz, ROWS, LANES), F32),
            pltpu.VMEM((ny, nz, ROWS, LANES), F32),
            pltpu.VMEM((ny, nz, ROWS // 2, LANES), F32),
            pltpu.VMEM((nz, ny, ROWS // 2, LANES), F32),
            pltpu.VMEM((ny, nz, ROWS // 2, LANES), F32),
            pltpu.VMEM((nz, ROWS // 2, LANES), F32),
            pltpu.VMEM((nz, ny, ROWS // 2, LANES), F32),
            pltpu.VMEM((ny, ROWS // 2, LANES), F32),
            pltpu.VMEM((groups * LANES, wide), BF16),
            pltpu.VMEM((ROWS, groups * LANES), BF16),
            dma((6,)),
            dma((2, 3, nyh, 2)), dma((2, 3, nyh, 2)),
            dma((2, 2)), dma((2, 2)),
            dma((ny,)), dma((ny,)),
            dma((ny,)), dma((ny,)),
            dma((nz,)), dma((nz,)),
            dma((nz,)), dma((nz,)),
            dma((ny,)), dma((ny,)),
            dma((groups,)), dma((groups,)),
            dma((ny,)), dma((ny,)),
            dma, dma((2, nz // 2 + 1, ny)),
            dma, dma((nz,)), dma,
            dma, dma((2, nz // 2 + 1)), dma, dma((ny,)), dma, dma((ny,)), dma,
        ],
        compiler_params=pltpu.CompilerParams(
            collective_id=0, has_side_effects=True, vmem_limit_bytes=58 * 1024 * 1024
        ),
        cost_estimate=pl.CostEstimate(
            flops=2 * tokens * LANES * (groups * wide + nz * ny * nc * ROWS),
            bytes_accessed=16 * 1024 * 1024,
            transcendentals=ROWS * LANES,
        ),
        name="galore_step",
    )(acts, grad_out, basis, master, exp_avg, exp_avg_sq)
    new_master, weight, new_avg, new_avg_sq = pl.pallas_call(
        deliver,
        out_shape=[shape(r.shape, r.dtype) for r in results],
        in_specs=[hbm] * 4,
        out_specs=[hbm] * 4,
        scratch_shapes=[pltpu.VMEM(results[i].shape, results[i].dtype) for i in (1, 0, 2, 3)]
        + [dma((2, 3 + nz))],
        compiler_params=pltpu.CompilerParams(vmem_limit_bytes=58 * 1024 * 1024),
        name="deliver",
    )(*results)
    return new_master, weight.reshape(nz * ny * nc * ROWS, wide), new_avg, new_avg_sq


def build(mesh, sizes):
    return jax.shard_map(
        functools.partial(on_device, sizes),
        mesh=mesh,
        in_specs=(
            P("dp", "fsdp"),
            P("dp", None),
            P("fsdp", None),
            P("dp", "fsdp"),
            P("dp", "fsdp"),
            P("dp", "fsdp"),
        ),
        out_specs=(P("dp", "fsdp"), P(None, "fsdp"), P("dp", "fsdp"), P("dp", "fsdp")),
        check_vma=False,
    )


def solution(mesh):
    return build(mesh, (16, 4, 2, 2, 4))
```
